32 devices in a mesh: group: 2 (over x), lat: 16 (over z, y, core).
Axes of the slice: x: 2, y: 2, z: 4, core: 2. Of those that a mesh axis runs over, the one named last changes fastest.
Arguments:
- grad_out: bfloat16 [128, 3, 2048], P(('group', 'lat')), parts along dimension 0, may hold values from -6 to 6
- layer_inputs: bfloat16 [128, 3, 2048], P(('group', 'lat')), parts along dimension 0, may hold values from -6 to 6
- active: int32 [128, 3, 16384], P('group', None, 'lat'), parts along dimension 0, may hold values 0 or 1
- enc_weight: bfloat16 [3, 2048, 16384], P(None, None, 'lat'), may hold values from -0.046875 to 0.046875
- dec_weight: bfloat16 [6, 16384, 2048], P(None, 'lat'), may hold values from -0.125 to 0.125
Outputs:
- enc_grad: bfloat16 [6, 2048, 16384], P('group', None, 'lat'), parts along dimension 0
- input_grad: bfloat16 [128, 3, 2048], P(('group', 'lat')), parts along dimension 0
The draws below stay inside these ranges and needn't reach their ends.
There are 2 independent parts, one for each index of `group`. The reference program is written for one: setup_inputs(seed, part) draws one part's arguments, and reference() takes and returns one part's arrays. A program takes and returns all parts, laid end to end along the dimension named above; an argument that names none is the same for every part. Nothing has to cross between parts.
All inputs are finite; a program needn't handle non-finite values. No bound on the sum of `active` on one device may be relied on, other than what follows from the above.
Results may differ from the reference program's by a relative error of at most 0.0049.
Values may be sent and summed in bfloat16 or wider, within the bound.
A program may use at most 128 MiB of HBM per device.

```python
import jax
import jax.numpy as jnp
from jax import lax

D = 2048
F = 16384
LAYERS = 3
TOKENS = 64
PAIRS = 6


def plant(values, stream_key, least, largest):
    extent = values.shape
    place = [jax.random.randint(jax.random.fold_in(stream_key, axis), (), 0, extent[axis]) for axis in range(len(extent))]
    values = values.at[tuple(place)].set(least)
    longest = extent.index(max(extent))
    place[longest] = (place[longest] + 1) % extent[longest]
    return values.at[tuple(place)].set(largest)


def steps_of(key, shape, shards, low, largest):
    gain = 1.0
    for axis_at, parts in shards:
        draws = jax.random.uniform(jax.random.fold_in(jax.random.fold_in(key, 6), axis_at), (parts,), jnp.float32, low / len(shards), largest / len(shards))
        gain = gain * jnp.repeat(jnp.exp(draws), shape[axis_at] // parts).reshape((-1,) + (1,) * (len(shape) - 1 - axis_at))
    return gain


def bell_draw(own_key, dims, deviation, most, shards=(), dtype=jnp.bfloat16):
    array = deviation * jax.random.normal(own_key, dims, jnp.float32)
    if shards:
        array = array * steps_of(own_key, dims, shards, -0.22, 0.18)
    return jnp.clip(array, -most, most).astype(dtype)


def setup_inputs(seed: int = 0, part: int = 0) -> dict:
    streams_of = jax.random.split(jax.random.key(seed), 6)
    own_keys = jax.random.split(jax.random.fold_in(streams_of[5], part), 6)
    return {
        "grad_out": bell_draw(own_keys[0], (TOKENS, LAYERS, D), 1.0, 6.0, ((0, 16),)),
        "layer_inputs": bell_draw(own_keys[1], (TOKENS, LAYERS, D), 1.0, 6.0, ((0, 16),)),
        "active": plant((jax.random.randint(own_keys[2], (TOKENS, LAYERS, F), 0, 3) < 1).astype(jnp.int32), jax.random.fold_in(own_keys[2], 1), 0, 1),
        "enc_weight": bell_draw(streams_of[3], (LAYERS, D, F), F ** -0.5, 0.046875, ((2, 16),)),
        "dec_weight": bell_draw(streams_of[4], (PAIRS, F, D), D ** -0.5, 0.125, ((1, 16),)),
    }


def pair_index(source, target, layers):
    return source * layers - source * (source - 1) // 2 + target - source


def reference(grad_out, layer_inputs, active, enc_weight, dec_weight):
    columns = []
    for source in range(LAYERS):
        total = jnp.zeros((TOKENS, F), jnp.float32)
        for target in range(source, LAYERS):
            weight = dec_weight[pair_index(source, target, LAYERS)]
            total = total + jnp.dot(grad_out[:, target, :], weight.T, preferred_element_type=jnp.float32)
        gates = active[:, source, :].astype(jnp.float32)
        columns.append((total * gates).astype(jnp.bfloat16))
    pre_grad = jnp.stack(columns, axis=1)
    enc_total = jnp.einsum("rld,rlf->ldf", layer_inputs.astype(jnp.float32), pre_grad.astype(jnp.float32), precision=lax.Precision.HIGHEST)
    enc_grad = (enc_total * (TOKENS ** -0.5)).astype(jnp.bfloat16)
    summed = jnp.einsum("rlf,ldf->rld", pre_grad.astype(jnp.float32), enc_weight.astype(jnp.float32), precision=lax.Precision.HIGHEST)
    return enc_grad, summed.astype(jnp.bfloat16)
```

```python
import functools

import jax
import jax.numpy as jnp
from jax import lax
from jax.experimental import pallas as pl
from jax.experimental.pallas import tpu as pltpu
from jax.sharding import PartitionSpec as P

MESH = pl.DeviceIdType.MESH
F32 = jnp.float32
BF16 = jnp.bfloat16
NT = (((1,), (1,)), ((), ()))
TN = (((0,), (0,)), ((), ()))


def pair_index(source, target, layers):
    return source * layers - source * (source - 1) // 2 + target - source


def natural_of(index):
    q = index >> 6
    hh = (index >> 4) & 3
    y = (index >> 3) & 1
    c = (index >> 2) & 1
    r = index & 3
    return (c * 2 + y) * 64 + hh * 16 + r * 4 + q


def exchange_kernel(
    n, layers, rows, width,
    g_ref, x_ref, act_hbm, enc_hbm, dec_hbm,
    pre_hbm, xg_hbm, ig_ref,
    act_v, enc_v, dec_v, own32, out32, mask_v, gat, nat, pre_v, stage,
    s1, r1, keep, s2, r2, s3, r3, perm, perm_t,
    w_sem, o_sem, zs, zr, ys, yr, cs, cr, s1s, s1r, s2s, s2r, s3s, s3r,
):
    high = n // 4
    groups = n // 16
    tokens = rows * n
    q_width = width // 4
    local = enc_v.shape[2]
    tile = 256
    me = lax.axis_index("lat")
    group = lax.axis_index("group")
    c = me % 2
    y = (me // 2) % 2
    h = me // 4
    l_mine = c * 2 + y
    core_peer = me + 1 - 2 * c
    y_peer = me + 2 - 4 * y
    z_peers = [((h + j) % high) * 4 + me % 4 for j in range(1, high)]

    weight = {}
    count = 0

    def load(src, dst):
        nonlocal count
        copy = pltpu.make_async_copy(src, dst, w_sem.at[count])
        copy.start()
        count += 1
        return copy

    barrier = pltpu.get_barrier_semaphore()
    for peer in z_peers + [y_peer, core_peer]:
        pl.semaphore_signal(barrier, inc=1, device_id=(group, peer), device_id_type=MESH)

    act_copy = load(act_hbm, act_v)
    for source in reversed(range(layers)):
        for target in range(source, layers):
            p = pair_index(source, target, layers)
            weight["dec", p] = load(dec_hbm.at[p], dec_v.at[p])
        weight["enc", source] = load(enc_hbm.at[source], enc_v.at[source])

    for a, ref in enumerate((g_ref, x_ref)):
        for r in range(rows):
            value = ref[r].astype(F32)
            for t in range(layers):
                for q in range(4):
                    own32[a * layers + t, pl.ds(r * 4 + q, 1), :] = value[t : t + 1, q * q_width : (q + 1) * q_width]
    for k in range(2 * layers):
        gat.at[k, l_mine, h][...] = own32[k].astype(BF16)

    pl.semaphore_wait(barrier, len(z_peers) + 2)

    def remote(src, dst, send, recv, peer):
        copy = pltpu.make_async_remote_copy(
            src_ref=src, dst_ref=dst, send_sem=send, recv_sem=recv,
            device_id=(group, peer), device_id_type=MESH,
        )
        copy.start()
        return copy

    sent = []
    z_of, y_of, c_of = {}, {}, {}

    def z_start(k):
        z_of[k] = [
            remote(gat.at[k, l_mine, h], gat.at[k, l_mine, h], zs.at[k, j], zr.at[k, j], peer)
            for j, peer in enumerate(z_peers)
        ]
        sent.extend(z_of[k])

    def y_start(k):
        for copy in z_of[k]:
            copy.wait_recv()
        y_of[k] = remote(gat.at[k, l_mine], gat.at[k, l_mine], ys.at[k], yr.at[k], y_peer)
        sent.append(y_of[k])

    def c_start(k):
        y_of[k].wait_recv()
        c_of[k] = remote(
            gat.at[k, pl.ds(c * 2, 2)], gat.at[k, pl.ds(c * 2, 2)], cs.at[k], cr.at[k], core_peer
        )
        sent.append(c_of[k])

    def gathered(k):
        c_of[k].wait_recv()
        for gi in range(groups):
            block = gat[k, :, pl.ds(gi * 4, 4)].reshape(256, q_width)
            moved = jnp.dot(perm[...], block, preferred_element_type=F32).astype(BF16)
            for q in range(4):
                nat[k, pl.ds(gi * 64, 64), pl.ds(q * q_width, q_width)] = moved[q * 64 : (q + 1) * 64]

    order = list(reversed(range(layers)))
    for t in order:
        z_start(t)

    row = lax.broadcasted_iota(jnp.int32, (256, 256), 0)
    col = lax.broadcasted_iota(jnp.int32, (256, 256), 1)
    perm[...] = jnp.where(natural_of(row) == col, 1.0, 0.0).astype(BF16)
    perm_t[...] = jnp.where(natural_of(col) == row, 1.0, 0.0).astype(BF16)
    act_copy.wait()
    for s in order:
        mask_v[s] = act_v[:, s, :].astype(F32)

    def source_grad(s):
        pairs = [pair_index(s, t, layers) for t in range(s, layers)]
        for p in pairs:
            weight["dec", p].wait()

        def body(i, carry):
            cols = pl.ds(pl.multiple_of(i * tile, tile), tile)
            total = jnp.zeros((tokens, tile), F32)
            for t, p in zip(range(s, layers), pairs):
                total = total + lax.dot_general(nat[t], dec_v[p, cols, :], NT, preferred_element_type=F32)
            pre_v[s, :, cols] = (total * mask_v[s, :, cols]).astype(BF16)
            return carry

        lax.fori_loop(0, local // tile, body, 0)

    out_copies = []

    def save(src, dst):
        copy = pltpu.make_async_copy(src, dst, o_sem.at[len(out_copies)])
        copy.start()
        out_copies.append(copy)

    first, second, third = {}, {}, {}

    def input_partial(s):
        weight["enc", s].wait()

        def body(q, carry):
            deep = pl.ds(pl.multiple_of(q * q_width, q_width), q_width)
            part = lax.dot_general(pre_v[s], enc_v[s, deep, :], NT, preferred_element_type=F32).astype(BF16)
            for gi in range(groups):
                stage[s, gi, q] = part[gi * 64 : (gi + 1) * 64]
            return carry

        lax.fori_loop(0, 4, body, 0)
        for gi in range(groups):
            block = stage[s, gi].reshape(256, q_width)
            moved = jnp.dot(perm_t[...], block, preferred_element_type=F32).astype(BF16)
            s1[s, :, pl.ds(gi * 4, 4)] = moved.reshape(4, 4, 16, q_width)
        first[s] = remote(s1.at[s, pl.ds(2 - c * 2, 2)], r1.at[s], s1s.at[s], s1r.at[s], core_peer)
        sent.append(first[s])

    def reduce_y(s):
        first[s].wait_recv()
        s2[s] = (s1[s, c * 2 + 1 - y].astype(F32) + r1[s, 1 - y].astype(F32)).astype(BF16)
        second[s] = remote(s2.at[s], r2.at[s], s2s.at[s], s2r.at[s], y_peer)
        sent.append(second[s])
        keep[s] = s1[s, l_mine].astype(F32) + r1[s, y].astype(F32)

    def reduce_z(s):
        second[s].wait_recv()
        total = keep[s] + r2[s].astype(F32)
        keep[s] = total
        s3[s] = total.astype(BF16)
        third[s] = [
            remote(s3.at[s, (h + j + 1) % high], r3.at[s, j], s3s.at[s, j], s3r.at[s, j], peer)
            for j, peer in enumerate(z_peers)
        ]
        sent.extend(third[s])

    def finish(s):
        total = keep[s, h]
        for j, copy in enumerate(third[s]):
            copy.wait_recv()
            total = total + r3[s, j].astype(F32)
        for r in range(rows):
            for q in range(4):
                out32[r, pl.ds(s, 1), pl.ds(q * q_width, q_width)] = total[r * 4 + q : r * 4 + q + 1]

    def x_ready(k):
        gathered(k)
        save(nat.at[k], xg_hbm.at[k - layers])

    hidden = []
    for t in order:
        y_start(t)
    for t in order:
        c_start(t)
        z_start(layers + t)
    for i, s in enumerate(order):
        gathered(s)
        source_grad(s)
        save(pre_v.at[s], pre_hbm.at[s])
        y_start(layers + s)
        if i >= 1:
            reduce_y(order[i - 1])
        input_partial(s)
        if i >= 1:
            reduce_z(order[i - 1])
            c_start(layers + order[i - 1])
        if i >= 2:
            finish(order[i - 2])
            x_ready(layers + order[i - 2])
    last = order[-1]
    reduce_y(last)
    c_start(layers + last)
    for s in order[:-1][-1:]:
        finish(s)
        x_ready(layers + s)
    reduce_z(last)
    x_ready(layers + last)
    finish(last)
    ig_ref[...] = out32[...].astype(BF16)
    for copy in out_copies:
        copy.wait()
    for copy in sent:
        copy.wait_send()


def outer_kernel(scale, x_ref, pre_ref, out_ref):
    out_ref[0] = (lax.dot_general(x_ref[0], pre_ref[0], TN, preferred_element_type=F32) * scale).astype(BF16)


def per_device(n, grad_out, layer_inputs, active, enc_weight, dec_weight):
    rows, layers, width = grad_out.shape
    local = enc_weight.shape[2]
    tokens = rows * n
    high = n // 4
    q_width = width // 4
    dma = pltpu.SemaphoreType.DMA
    pairs = dec_weight.shape[0]
    any_space = pl.BlockSpec(memory_space=pl.ANY)
    vmem = pl.BlockSpec(memory_space=pltpu.VMEM)
    macs = tokens * local * width * (pairs + layers)
    pre, xg, input_grad = pl.pallas_call(
        functools.partial(exchange_kernel, n, layers, rows, width),
        out_shape=(
            jax.ShapeDtypeStruct((layers, tokens, local), BF16),
            jax.ShapeDtypeStruct((layers, tokens, width), BF16),
            jax.ShapeDtypeStruct((rows, layers, width), BF16),
        ),
        in_specs=[vmem, vmem, any_space, any_space, any_space],
        out_specs=(any_space, any_space, vmem),
        scratch_shapes=[
            pltpu.VMEM((tokens, layers, local), jnp.int32),
            pltpu.VMEM((layers, width, local), BF16),
            pltpu.VMEM((pairs, local, width), BF16),
            pltpu.VMEM((2 * layers, 16, q_width), F32),
            pltpu.VMEM((rows, layers, width), F32),
            pltpu.VMEM((layers, tokens, local), F32),
            pltpu.VMEM((2 * layers, 4, high, 16, q_width), BF16),
            pltpu.VMEM((2 * layers, tokens, width), BF16),
            pltpu.VMEM((layers, tokens, local), BF16),
            pltpu.VMEM((layers, n // 16, 4, 64, q_width), BF16),
            pltpu.VMEM((layers, 4, high, 16, q_width), BF16),
            pltpu.VMEM((layers, 2, high, 16, q_width), BF16),
            pltpu.VMEM((layers, high, 16, q_width), F32),
            pltpu.VMEM((layers, high, 16, q_width), BF16),
            pltpu.VMEM((layers, high, 16, q_width), BF16),
            pltpu.VMEM((layers, high, 16, q_width), BF16),
            pltpu.VMEM((layers, high - 1, 16, q_width), BF16),
            pltpu.VMEM((256, 256), BF16),
            pltpu.VMEM((256, 256), BF16),
            dma((1 + pairs + layers,)),
            dma((2 * layers,)),
            dma((2 * layers, high - 1)),
            dma((2 * layers, high - 1)),
            dma((2 * layers,)),
            dma((2 * layers,)),
            dma((2 * layers,)),
            dma((2 * layers,)),
            dma((layers,)),
            dma((layers,)),
            dma((layers,)),
            dma((layers,)),
            dma((layers, high - 1)),
            dma((layers, high - 1)),
        ],
        compiler_params=pltpu.CompilerParams(
            collective_id=0, has_side_effects=True, vmem_limit_bytes=60 * 1024 * 1024
        ),
        cost_estimate=pl.CostEstimate(
            flops=2 * macs,
            bytes_accessed=2 * local * width * (pairs + layers),
            transcendentals=0,
        ),
    )(grad_out, layer_inputs, active, enc_weight, dec_weight)

    deep = 512
    enc_grad = pl.pallas_call(
        functools.partial(outer_kernel, tokens ** (-0.5)),
        grid=(layers, width // deep),
        in_specs=[
            pl.BlockSpec((1, tokens, deep), lambda l, d: (l, 0, d)),
            pl.BlockSpec((1, tokens, local), lambda l, d: (l, 0, 0)),
        ],
        out_specs=pl.BlockSpec((1, deep, local), lambda l, d: (l, d, 0)),
        out_shape=jax.ShapeDtypeStruct((layers, width, local), BF16),
        compiler_params=pltpu.CompilerParams(vmem_limit_bytes=32 * 1024 * 1024),
        cost_estimate=pl.CostEstimate(
            flops=2 * tokens * local * width * layers,
            bytes_accessed=2 * local * width * layers,
            transcendentals=0,
        ),
    )(xg, pre)
    return enc_grad, input_grad


def solution(mesh):
    return jax.shard_map(
        functools.partial(per_device, mesh.shape["lat"]),
        mesh=mesh,
        in_specs=(
            P(("group", "lat"), None, None),
            P(("group", "lat"), None, None),
            P("group", None, "lat"),
            P(None, None, "lat"),
            P(None, "lat", None),
        ),
        out_specs=(P("group", None, "lat"), P(("group", "lat"), None, None)),
        check_vma=False,
    )
```

```python
import functools

import jax
import jax.numpy as jnp
from jax import lax
from jax.experimental import pallas as pl
from jax.experimental.pallas import tpu as pltpu
from jax.sharding import PartitionSpec as P

MESH = pl.DeviceIdType.MESH
F32 = jnp.float32
BF16 = jnp.bfloat16
NT = (((1,), (1,)), ((), ()))
TN = (((0,), (0,)), ((), ()))


def pair_index(source, target, layers):
    return source * layers - source * (source - 1) // 2 + target - source


def natural_of(index):
    q = index >> 6
    hh = (index >> 4) & 3
    y = (index >> 3) & 1
    c = (index >> 2) & 1
    r = index & 3
    return (c * 2 + y) * 64 + hh * 16 + q * 4 + r


def exchange_kernel(
    n, layers, rows, width,
    g_ref, x_ref, act_hbm, enc_hbm, dec_hbm,
    pre_hbm, xg_hbm, ig_ref,
    act_v, enc_v, dec_v, own32, gat, nat, pre_v, stage,
    s1, r1, keep, s2, r2, s3, r3, perm, perm_t,
    w_sem, o_sem, zs, zr, ys, yr, cs, cr, s1s, s1r, s2s, s2r, s3s, s3r,
):
    high = n // 4
    groups = n // 16
    tokens = rows * n
    q_width = width // 4
    local = enc_v.shape[2]
    tile = min(512, local)
    me = lax.axis_index("lat")
    group = lax.axis_index("group")
    c = me % 2
    y = (me // 2) % 2
    h = me // 4
    l_mine = c * 2 + y
    core_peer = me + 1 - 2 * c
    y_peer = me + 2 - 4 * y
    z_peers = [((h + j) % high) * 4 + me % 4 for j in range(1, high)]

    weight = {}
    count = 0

    def load(src, dst):
        nonlocal count
        copy = pltpu.make_async_copy(src, dst, w_sem.at[count])
        copy.start()
        count += 1
        return copy

    barrier = pltpu.get_barrier_semaphore()
    for peer in z_peers + [y_peer, core_peer]:
        pl.semaphore_signal(barrier, inc=1, device_id=(group, peer), device_id_type=MESH)

    act_copy = load(act_hbm, act_v)
    for source in reversed(range(layers)):
        for target in range(source, layers):
            p = pair_index(source, target, layers)
            weight["dec", p] = load(dec_hbm.at[p], dec_v.at[p])
        weight["enc", source] = load(enc_hbm.at[source], enc_v.at[source])

    for a, ref in enumerate((g_ref, x_ref)):
        for t in range(layers):
            value = ref[t].astype(F32)
            for q in range(4):
                own32[a * layers + t, pl.ds(q * rows, rows), :] = value[:, q * q_width : (q + 1) * q_width]
    for k in range(2 * layers):
        gat.at[k, l_mine, h][...] = own32[k].astype(BF16)

    pl.semaphore_wait(barrier, len(z_peers) + 2)

    def remote(src, dst, send, recv, peer):
        copy = pltpu.make_async_remote_copy(
            src_ref=src, dst_ref=dst, send_sem=send, recv_sem=recv,
            device_id=(group, peer), device_id_type=MESH,
        )
        copy.start()
        return copy

    sent = []
    z_of, y_of, c_of = {}, {}, {}

    def z_start(k):
        z_of[k] = [
            remote(gat.at[k, l_mine, h], gat.at[k, l_mine, h], zs.at[k, j], zr.at[k, j], peer)
            for j, peer in enumerate(z_peers)
        ]
        sent.extend(z_of[k])

    def y_start(k):
        for copy in z_of[k]:
            copy.wait_recv()
        y_of[k] = remote(gat.at[k, l_mine], gat.at[k, l_mine], ys.at[k], yr.at[k], y_peer)
        sent.append(y_of[k])

    def c_start(k):
        y_of[k].wait_recv()
        c_of[k] = remote(
            gat.at[k, pl.ds(c * 2, 2)], gat.at[k, pl.ds(c * 2, 2)], cs.at[k], cr.at[k], core_peer
        )
        sent.append(c_of[k])

    def gathered(k):
        c_of[k].wait_recv()
        for gi in range(groups):
            block = gat[k, :, pl.ds(gi * 4, 4)].reshape(256, q_width)
            moved = jnp.dot(perm[...], block, preferred_element_type=F32).astype(BF16)
            for q in range(4):
                nat[k, pl.ds(gi * 64, 64), pl.ds(q * q_width, q_width)] = moved[q * 64 : (q + 1) * 64]

    order = list(reversed(range(layers)))
    for t in order:
        z_start(t)

    row = lax.broadcasted_iota(jnp.int32, (256, 256), 0)
    col = lax.broadcasted_iota(jnp.int32, (256, 256), 1)
    perm[...] = jnp.where(natural_of(row) == col, 1.0, 0.0).astype(BF16)
    perm_t[...] = jnp.where(natural_of(col) == row, 1.0, 0.0).astype(BF16)
    act_copy.wait()

    def source_grad(s):
        pairs = [pair_index(s, t, layers) for t in range(s, layers)]
        for p in pairs:
            weight["dec", p].wait()

        def body(i, carry):
            cols = pl.ds(pl.multiple_of(i * tile, tile), tile)
            total = jnp.zeros((tokens, tile), F32)
            for t, p in zip(range(s, layers), pairs):
                total = total + lax.dot_general(nat[t], dec_v[p, cols, :], NT, preferred_element_type=F32)
            pre_v[s, :, cols] = (total * act_v[s, :, cols].astype(F32)).astype(BF16)
            return carry

        lax.fori_loop(0, local // tile, body, 0)

    out_copies = []

    def save(src, dst):
        copy = pltpu.make_async_copy(src, dst, o_sem.at[len(out_copies)])
        copy.start()
        out_copies.append(copy)

    first, second, third = {}, {}, {}

    def input_partial(s):
        weight["enc", s].wait()

        def body(q, carry):
            deep = pl.ds(pl.multiple_of(q * q_width, q_width), q_width)
            part = lax.dot_general(pre_v[s], enc_v[s, deep, :], NT, preferred_element_type=F32).astype(BF16)
            for gi in range(groups):
                stage[s, gi, q] = part[gi * 64 : (gi + 1) * 64]
            return carry

        lax.fori_loop(0, 4, body, 0)
        for gi in range(groups):
            block = stage[s, gi].reshape(256, q_width)
            moved = jnp.dot(perm_t[...], block, preferred_element_type=F32).astype(BF16)
            s1[s, :, pl.ds(gi * 4, 4)] = moved.reshape(4, 4, 16, q_width)
        first[s] = remote(s1.at[s, pl.ds(2 - c * 2, 2)], r1.at[s], s1s.at[s], s1r.at[s], core_peer)
        sent.append(first[s])

    def reduce_y(s):
        first[s].wait_recv()
        s2[s] = (s1[s, c * 2 + 1 - y].astype(F32) + r1[s, 1 - y].astype(F32)).astype(BF16)
        second[s] = remote(s2.at[s], r2.at[s], s2s.at[s], s2r.at[s], y_peer)
        sent.append(second[s])
        keep[s] = s1[s, l_mine].astype(F32) + r1[s, y].astype(F32)

    def reduce_z(s):
        second[s].wait_recv()
        total = keep[s] + r2[s].astype(F32)
        keep[s] = total
        s3[s] = total.astype(BF16)
        third[s] = [
            remote(s3.at[s, (h + j + 1) % high], r3.at[s, j], s3s.at[s, j], s3r.at[s, j], peer)
            for j, peer in enumerate(z_peers)
        ]
        sent.extend(third[s])

    def finish(s):
        total = keep[s, h]
        for j, copy in enumerate(third[s]):
            copy.wait_recv()
            total = total + r3[s, j].astype(F32)
        for q in range(4):
            ig_ref[s, :, pl.ds(q * q_width, q_width)] = total[q * rows : (q + 1) * rows].astype(BF16)

    def x_ready(k):
        gathered(k)
        save(nat.at[k], xg_hbm.at[k - layers])

    for t in order:
        y_start(t)
    for t in order:
        z_start(layers + t)
    for t in order:
        c_start(t)
    extra = {"y": 0, "c": 0}

    def x_step(kind, many):
        for _ in range(many):
            if extra[kind] < layers:
                (y_start if kind == "y" else c_start)(layers + order[extra[kind]])
                extra[kind] += 1

    for i, s in enumerate(order):
        last = i == layers - 1
        gathered(s)
        if last:
            x_step("y", layers)
        source_grad(s)
        save(pre_v.at[s], pre_hbm.at[s])
        if i >= 2:
            reduce_z(order[i - 2])
        if i >= 1:
            reduce_y(order[i - 1])
            x_step("y", 1)
        if last:
            x_step("c", 1)
        input_partial(s)
    s = order[-1]
    x_step("c", 1)
    reduce_y(s)
    x_step("c", layers)
    if layers >= 2:
        reduce_z(order[-2])
    for t in order[:-1]:
        x_ready(layers + t)
    reduce_z(s)
    x_ready(layers + s)
    for t in order:
        finish(t)
    for copy in out_copies:
        copy.wait()
    for copy in sent:
        copy.wait_send()


def outer_kernel(scale, x_ref, pre_ref, out_ref):
    out_ref[0] = (lax.dot_general(x_ref[0], pre_ref[0], TN, preferred_element_type=F32) * scale).astype(BF16)


def per_device(n, grad_out, layer_inputs, active, enc_weight, dec_weight):
    rows, layers, width = grad_out.shape
    local = enc_weight.shape[2]
    tokens = rows * n
    high = n // 4
    q_width = width // 4
    dma = pltpu.SemaphoreType.DMA
    pairs = dec_weight.shape[0]
    any_space = pl.BlockSpec(memory_space=pl.ANY)
    vmem = pl.BlockSpec(memory_space=pltpu.VMEM)
    macs = tokens * local * width * (pairs + layers)
    pre, xg, input_grad = pl.pallas_call(
        functools.partial(exchange_kernel, n, layers, rows, width),
        out_shape=(
            jax.ShapeDtypeStruct((layers, tokens, local), BF16),
            jax.ShapeDtypeStruct((layers, tokens, width), BF16),
            jax.ShapeDtypeStruct((layers, rows, width), BF16),
        ),
        in_specs=[vmem, vmem, any_space, any_space, any_space],
        out_specs=(any_space, any_space, vmem),
        scratch_shapes=[
            pltpu.VMEM((layers, tokens, local), jnp.int32),
            pltpu.VMEM((layers, width, local), BF16),
            pltpu.VMEM((pairs, local, width), BF16),
            pltpu.VMEM((2 * layers, 16, q_width), F32),
            pltpu.VMEM((2 * layers, 4, high, 16, q_width), BF16),
            pltpu.VMEM((2 * layers, tokens, width), BF16),
            pltpu.VMEM((layers, tokens, local), BF16),
            pltpu.VMEM((layers, n // 16, 4, 64, q_width), BF16),
            pltpu.VMEM((layers, 4, high, 16, q_width), BF16),
            pltpu.VMEM((layers, 2, high, 16, q_width), BF16),
            pltpu.VMEM((layers, high, 16, q_width), F32),
            pltpu.VMEM((layers, high, 16, q_width), BF16),
            pltpu.VMEM((layers, high, 16, q_width), BF16),
            pltpu.VMEM((layers, high, 16, q_width), BF16),
            pltpu.VMEM((layers, high - 1, 16, q_width), BF16),
            pltpu.VMEM((256, 256), BF16),
            pltpu.VMEM((256, 256), BF16),
            dma((1 + pairs + layers,)),
            dma((2 * layers,)),
            dma((2 * layers, high - 1)),
            dma((2 * layers, high - 1)),
            dma((2 * layers,)),
            dma((2 * layers,)),
            dma((2 * layers,)),
            dma((2 * layers,)),
            dma((layers,)),
            dma((layers,)),
            dma((layers,)),
            dma((layers,)),
            dma((layers, high - 1)),
            dma((layers, high - 1)),
        ],
        compiler_params=pltpu.CompilerParams(
            collective_id=0, has_side_effects=True, vmem_limit_bytes=60 * 1024 * 1024
        ),
        cost_estimate=pl.CostEstimate(
            flops=2 * macs,
            bytes_accessed=2 * local * width * (pairs + layers),
            transcendentals=0,
        ),
    )(
        grad_out.transpose(1, 0, 2),
        layer_inputs.transpose(1, 0, 2),
        active.transpose(1, 0, 2),
        enc_weight,
        dec_weight,
    )

    deep = width // 2
    enc_grad = pl.pallas_call(
        functools.partial(outer_kernel, tokens ** (-0.5)),
        grid=(layers, width // deep),
        in_specs=[
            pl.BlockSpec((1, tokens, deep), lambda l, d: (l, 0, d)),
            pl.BlockSpec((1, tokens, local), lambda l, d: (l, 0, 0)),
        ],
        out_specs=pl.BlockSpec((1, deep, local), lambda l, d: (l, d, 0)),
        out_shape=jax.ShapeDtypeStruct((layers, width, local), BF16),
        compiler_params=pltpu.CompilerParams(vmem_limit_bytes=60 * 1024 * 1024),
        cost_estimate=pl.CostEstimate(
            flops=2 * tokens * local * width * layers,
            bytes_accessed=2 * local * width * layers,
            transcendentals=0,
        ),
    )(xg, pre)
    return enc_grad, input_grad.transpose(1, 0, 2)


def solution(mesh):
    return jax.shard_map(
        functools.partial(per_device, mesh.shape["lat"]),
        mesh=mesh,
        in_specs=(
            P(("group", "lat"), None, None),
            P(("group", "lat"), None, None),
            P("group", None, "lat"),
            P(None, None, "lat"),
            P(None, "lat", None),
        ),
        out_specs=(P("group", None, "lat"), P(("group", "lat"), None, None)),
        check_vma=False,
    )
```

```python
import functools

import jax
import jax.numpy as jnp
from jax import lax
from jax.experimental import pallas as pl
from jax.experimental.pallas import tpu as pltpu
from jax.sharding import PartitionSpec as P

MESH = pl.DeviceIdType.MESH
F32 = jnp.float32
BF16 = jnp.bfloat16
NT = (((1,), (1,)), ((), ()))
TN = (((0,), (0,)), ((), ()))


def pair_index(source, target, layers):
    return source * layers - source * (source - 1) // 2 + target - source


def natural_of(index):
    q = index >> 6
    hh = (index >> 4) & 3
    y = (index >> 3) & 1
    c = (index >> 2) & 1
    r = index & 3
    return (c * 2 + y) * 64 + hh * 16 + q * 4 + r


def exchange_kernel(
    n, layers, rows, width,
    g_ref, x_ref, act_hbm, enc_hbm, dec_hbm,
    pre_hbm, xg_hbm, ig_ref,
    act_v, enc_v, dec_v, own32, gat, nat, pre_v, stage,
    s1, r1, keep, s2, r2, perm, perm_t,
    w_sem, o_sem, zs, zr, ys, yr, cs, cr, s1s, s1r, s2s, s2r,
):
    high = n // 4
    groups = n // 16
    tokens = rows * n
    q_width = width // 4
    local = enc_v.shape[2]
    tile = min(512, local)
    me = lax.axis_index("lat")
    group = lax.axis_index("group")
    c = me % 2
    y = (me // 2) % 2
    h = me // 4
    l_mine = c * 2 + y
    core_peer = me + 1 - 2 * c
    y_peer = me + 2 - 4 * y
    chip = me // 2
    chips = [(chip + m) % (2 * high) for m in range(1, 2 * high)]
    z_peers = [((h + j) % high) * 4 + me % 4 for j in range(1, high)]

    weight = {}
    count = 0

    def load(src, dst):
        nonlocal count
        copy = pltpu.make_async_copy(src, dst, w_sem.at[count])
        copy.start()
        count += 1
        return copy

    barrier = pltpu.get_barrier_semaphore()
    for peer in [w * 2 + c for w in chips] + [core_peer]:
        pl.semaphore_signal(barrier, inc=1, device_id=(group, peer), device_id_type=MESH)

    act_copy = load(act_hbm, act_v)
    for source in reversed(range(layers)):
        for target in range(source, layers):
            p = pair_index(source, target, layers)
            weight["dec", p] = load(dec_hbm.at[p], dec_v.at[p])
        weight["enc", source] = load(enc_hbm.at[source], enc_v.at[source])

    for a, ref in enumerate((g_ref, x_ref)):
        for t in range(layers):
            value = ref[t].astype(F32)
            for q in range(4):
                own32[a * layers + t, pl.ds(q * rows, rows), :] = value[:, q * q_width : (q + 1) * q_width]
    for k in range(2 * layers):
        gat.at[k, l_mine, h][...] = own32[k].astype(BF16)

    pl.semaphore_wait(barrier, len(chips) + 1)

    def remote(src, dst, send, recv, peer):
        copy = pltpu.make_async_remote_copy(
            src_ref=src, dst_ref=dst, send_sem=send, recv_sem=recv,
            device_id=(group, peer), device_id_type=MESH,
        )
        copy.start()
        return copy

    sent = []
    z_of, y_of, c_of = {}, {}, {}

    def z_start(k):
        z_of[k] = [
            remote(gat.at[k, l_mine, h], gat.at[k, l_mine, h], zs.at[k, j], zr.at[k, j], peer)
            for j, peer in enumerate(z_peers)
        ]
        sent.extend(z_of[k])

    def y_start(k):
        for copy in z_of[k]:
            copy.wait_recv()
        y_of[k] = remote(gat.at[k, l_mine], gat.at[k, l_mine], ys.at[k], yr.at[k], y_peer)
        sent.append(y_of[k])

    def c_start(k):
        y_of[k].wait_recv()
        c_of[k] = remote(
            gat.at[k, pl.ds(c * 2, 2)], gat.at[k, pl.ds(c * 2, 2)], cs.at[k], cr.at[k], core_peer
        )
        sent.append(c_of[k])

    def gathered(k):
        c_of[k].wait_recv()
        for gi in range(groups):
            block = gat[k, :, pl.ds(gi * 4, 4)].reshape(256, q_width)
            moved = jnp.dot(perm[...], block, preferred_element_type=F32).astype(BF16)
            for q in range(4):
                nat[k, pl.ds(gi * 64, 64), pl.ds(q * q_width, q_width)] = moved[q * 64 : (q + 1) * 64]

    order = list(reversed(range(layers)))
    for t in order:
        z_start(t)

    row = lax.broadcasted_iota(jnp.int32, (256, 256), 0)
    col = lax.broadcasted_iota(jnp.int32, (256, 256), 1)
    perm[...] = jnp.where(natural_of(row) == col, 1.0, 0.0).astype(BF16)
    perm_t[...] = jnp.where(natural_of(col) == row, 1.0, 0.0).astype(BF16)
    act_copy.wait()

    def source_grad(s):
        pairs = [pair_index(s, t, layers) for t in range(s, layers)]
        for p in pairs:
            weight["dec", p].wait()

        def body(i, carry):
            cols = pl.ds(pl.multiple_of(i * tile, tile), tile)
            total = jnp.zeros((tokens, tile), F32)
            for t, p in zip(range(s, layers), pairs):
                total = total + lax.dot_general(nat[t], dec_v[p, cols, :], NT, preferred_element_type=F32)
            pre_v[s, :, cols] = (total * act_v[s, :, cols].astype(F32)).astype(BF16)
            return carry

        lax.fori_loop(0, local // tile, body, 0)

    out_copies = []

    def save(src, dst):
        copy = pltpu.make_async_copy(src, dst, o_sem.at[len(out_copies)])
        copy.start()
        out_copies.append(copy)

    first, second = {}, {}

    def input_partial(s):
        weight["enc", s].wait()

        def body(q, carry):
            deep = pl.ds(pl.multiple_of(q * q_width, q_width), q_width)
            part = lax.dot_general(pre_v[s], enc_v[s, deep, :], NT, preferred_element_type=F32).astype(BF16)
            for gi in range(groups):
                stage[s, gi, q] = part[gi * 64 : (gi + 1) * 64]
            return carry

        lax.fori_loop(0, 4, body, 0)
        for gi in range(groups):
            block = stage[s, gi].reshape(256, q_width)
            moved = jnp.dot(perm_t[...], block, preferred_element_type=F32).astype(BF16)
            s1[s, :, pl.ds(gi * 4, 4)] = moved.reshape(4, 4, 16, q_width)
        first[s] = remote(s1.at[s, pl.ds(2 - c * 2, 2)], r1.at[s], s1s.at[s], s1r.at[s], core_peer)
        sent.append(first[s])

    def reduce_chip(s):
        first[s].wait_recv()
        s2[s] = (s1[s, pl.ds(c * 2, 2)].astype(F32) + r1[s].astype(F32)).astype(BF16)
        second[s] = [
            remote(s2.at[s, w % 2, w // 2], r2.at[s, m], s2s.at[s, m], s2r.at[s, m], w * 2 + c)
            for m, w in enumerate(chips)
        ]
        sent.extend(second[s])
        keep[s] = s1[s, l_mine, h].astype(F32) + r1[s, y, h].astype(F32)

    def finish(s):
        total = keep[s]
        for m, copy in enumerate(second[s]):
            copy.wait_recv()
            total = total + r2[s, m].astype(F32)
        for q in range(4):
            ig_ref[s, :, pl.ds(q * q_width, q_width)] = total[q * rows : (q + 1) * rows].astype(BF16)

    def x_ready(k):
        gathered(k)
        save(nat.at[k], xg_hbm.at[k - layers])

    for t in order:
        y_start(t)
    for t in order:
        z_start(layers + t)
    for t in order:
        c_start(t)
    extra = {"y": 0, "c": 0}

    def x_step(kind, many):
        for _ in range(many):
            if extra[kind] < layers:
                (y_start if kind == "y" else c_start)(layers + order[extra[kind]])
                extra[kind] += 1

    for i, s in enumerate(order):
        last = i == layers - 1
        gathered(s)
        if last:
            x_step("y", layers)
        source_grad(s)
        save(pre_v.at[s], pre_hbm.at[s])
        if i >= 1:
            reduce_chip(order[i - 1])
            x_step("y", 1)
        if last:
            x_step("c", 1)
        input_partial(s)
    s = order[-1]
    x_step("c", 1)
    reduce_chip(s)
    x_step("c", layers)
    for t in order:
        x_ready(layers + t)
    for t in order:
        finish(t)
    for copy in out_copies:
        copy.wait()
    for copy in sent:
        copy.wait_send()


def outer_kernel(scale, x_ref, pre_ref, out_hbm, out_v, sem):
    layers, width = out_v.shape[:2]
    deep = width // 2
    copies = []
    for l in range(layers):
        for d in range(0, width, deep):
            rows = pl.ds(d, deep)
            total = lax.dot_general(x_ref[l, :, rows], pre_ref[l], TN, preferred_element_type=F32)
            out_v[l, rows, :] = (total * scale).astype(BF16)
            copy = pltpu.make_async_copy(out_v.at[l, rows], out_hbm.at[l, rows], sem.at[len(copies)])
            copy.start()
            copies.append(copy)
    for copy in copies:
        copy.wait()


def per_device(n, grad_out, layer_inputs, active, enc_weight, dec_weight):
    rows, layers, width = grad_out.shape
    local = enc_weight.shape[2]
    tokens = rows * n
    high = n // 4
    q_width = width // 4
    dma = pltpu.SemaphoreType.DMA
    pairs = dec_weight.shape[0]
    any_space = pl.BlockSpec(memory_space=pl.ANY)
    vmem = pl.BlockSpec(memory_space=pltpu.VMEM)
    macs = tokens * local * width * (pairs + layers)
    pre, xg, input_grad = pl.pallas_call(
        functools.partial(exchange_kernel, n, layers, rows, width),
        out_shape=(
            jax.ShapeDtypeStruct((layers, tokens, local), BF16),
            jax.ShapeDtypeStruct((layers, tokens, width), BF16),
            jax.ShapeDtypeStruct((layers, rows, width), BF16),
        ),
        in_specs=[vmem, vmem, any_space, any_space, any_space],
        out_specs=(any_space, any_space, vmem),
        scratch_shapes=[
            pltpu.VMEM((layers, tokens, local), jnp.int32),
            pltpu.VMEM((layers, width, local), BF16),
            pltpu.VMEM((pairs, local, width), BF16),
            pltpu.VMEM((2 * layers, 16, q_width), F32),
            pltpu.VMEM((2 * layers, 4, high, 16, q_width), BF16),
            pltpu.VMEM((2 * layers, tokens, width), BF16),
            pltpu.VMEM((layers, tokens, local), BF16),
            pltpu.VMEM((layers, n // 16, 4, 64, q_width), BF16),
            pltpu.VMEM((layers, 4, high, 16, q_width), BF16),
            pltpu.VMEM((layers, 2, high, 16, q_width), BF16),
            pltpu.VMEM((layers, 16, q_width), F32),
            pltpu.VMEM((layers, 2, high, 16, q_width), BF16),
            pltpu.VMEM((layers, 2 * high - 1, 16, q_width), BF16),
            pltpu.VMEM((256, 256), BF16),
            pltpu.VMEM((256, 256), BF16),
            dma((1 + pairs + layers,)),
            dma((2 * layers,)),
            dma((2 * layers, high - 1)),
            dma((2 * layers, high - 1)),
            dma((2 * layers,)),
            dma((2 * layers,)),
            dma((2 * layers,)),
            dma((2 * layers,)),
            dma((layers,)),
            dma((layers,)),
            dma((layers, 2 * high - 1)),
            dma((layers, 2 * high - 1)),
        ],
        compiler_params=pltpu.CompilerParams(
            collective_id=0, has_side_effects=True, vmem_limit_bytes=60 * 1024 * 1024
        ),
        cost_estimate=pl.CostEstimate(
            flops=2 * macs,
            bytes_accessed=2 * local * width * (pairs + layers),
            transcendentals=0,
        ),
    )(
        grad_out.transpose(1, 0, 2),
        layer_inputs.transpose(1, 0, 2),
        active.transpose(1, 0, 2),
        enc_weight,
        dec_weight,
    )

    enc_grad = pl.pallas_call(
        functools.partial(outer_kernel, tokens ** (-0.5)),
        in_specs=[vmem, vmem],
        out_specs=any_space,
        scratch_shapes=[pltpu.VMEM((layers, width, local), BF16), dma((2 * layers,))],
        out_shape=jax.ShapeDtypeStruct((layers, width, local), BF16),
        compiler_params=pltpu.CompilerParams(vmem_limit_bytes=60 * 1024 * 1024),
        cost_estimate=pl.CostEstimate(
            flops=2 * tokens * local * width * layers,
            bytes_accessed=2 * local * width * layers,
            transcendentals=0,
        ),
    )(xg, pre)
    return enc_grad, input_grad.transpose(1, 0, 2)


def solution(mesh):
    return jax.shard_map(
        functools.partial(per_device, mesh.shape["lat"]),
        mesh=mesh,
        in_specs=(
            P(("group", "lat"), None, None),
            P(("group", "lat"), None, None),
            P("group", None, "lat"),
            P(None, None, "lat"),
            P(None, "lat", None),
        ),
        out_specs=(P("group", None, "lat"), P(("group", "lat"), None, None)),
        check_vma=False,
    )
```

```python
import functools

import jax
import jax.numpy as jnp
from jax import lax
from jax.experimental import pallas as pl
from jax.experimental.pallas import tpu as pltpu
from jax.sharding import PartitionSpec as P

MESH = pl.DeviceIdType.MESH
F32 = jnp.float32
BF16 = jnp.bfloat16
NT = (((1,), (1,)), ((), ()))
TN = (((0,), (0,)), ((), ()))


def pair_index(source, target, layers):
    return source * layers - source * (source - 1) // 2 + target - source


def natural_of(index):
    q = index >> 6
    hh = (index >> 4) & 3
    y = (index >> 3) & 1
    c = (index >> 2) & 1
    r = index & 3
    return (c * 2 + y) * 64 + hh * 16 + q * 4 + r


def exchange_kernel(
    n, layers, rows, width,
    g_ref, x_ref, act_hbm, enc_hbm, dec_hbm,
    pre_hbm, xg_hbm, ig_ref,
    act_v, enc_v, dec_v, own32, gat, nat, pre_v, stage,
    s1, r1, keep, s2, r2, perm, perm_t,
    w_sem, o_sem, zs, zr, ys, yr, cs, cr, s1s, s1r, s2s, s2r,
):
    high = n // 4
    groups = n // 16
    tokens = rows * n
    q_width = width // 4
    local = enc_v.shape[2]
    tile = min(512, local)
    me = lax.axis_index("lat")
    group = lax.axis_index("group")
    c = me % 2
    y = (me // 2) % 2
    h = me // 4
    l_mine = c * 2 + y
    core_peer = me + 1 - 2 * c
    y_peer = me + 2 - 4 * y
    chip = me // 2
    chips = [(chip + m) % (2 * high) for m in range(1, 2 * high)]
    z_peers = [((h + j) % high) * 4 + me % 4 for j in range(1, high)]

    weight = {}
    count = 0

    def load(src, dst):
        nonlocal count
        copy = pltpu.make_async_copy(src, dst, w_sem.at[count])
        copy.start()
        count += 1
        return copy

    barrier = pltpu.get_barrier_semaphore()
    for peer in [w * 2 + c for w in chips] + [core_peer]:
        pl.semaphore_signal(barrier, inc=1, device_id=(group, peer), device_id_type=MESH)

    act_copy = load(act_hbm, act_v)
    for source in reversed(range(layers)):
        for target in range(source, layers):
            p = pair_index(source, target, layers)
            weight["dec", p] = load(dec_hbm.at[p], dec_v.at[p])
        weight["enc", source] = load(enc_hbm.at[source], enc_v.at[source])

    for a, ref in enumerate((g_ref, x_ref)):
        for t in range(layers):
            value = ref[t].astype(F32)
            for q in range(4):
                own32[a * layers + t, pl.ds(q * rows, rows), :] = value[:, q * q_width : (q + 1) * q_width]
    for k in range(2 * layers):
        gat.at[k, l_mine, h][...] = own32[k].astype(BF16)

    pl.semaphore_wait(barrier, len(chips) + 1)

    def remote(src, dst, send, recv, peer):
        copy = pltpu.make_async_remote_copy(
            src_ref=src, dst_ref=dst, send_sem=send, recv_sem=recv,
            device_id=(group, peer), device_id_type=MESH,
        )
        copy.start()
        return copy

    sent = []
    second_unit = layers

    def unit(k):
        return pl.ds(k, layers if k == second_unit else 1)

    z_of, y_of, c_of = {}, {}, {}

    def z_start(k):
        z_of[k] = [
            remote(gat.at[unit(k), l_mine, h], gat.at[unit(k), l_mine, h], zs.at[k, j], zr.at[k, j], peer)
            for j, peer in enumerate(z_peers)
        ]
        sent.extend(z_of[k])

    def y_start(k):
        for copy in z_of[k]:
            copy.wait_recv()
        y_of[k] = remote(gat.at[unit(k), l_mine], gat.at[unit(k), l_mine], ys.at[k], yr.at[k], y_peer)
        sent.append(y_of[k])

    def c_start(k):
        y_of[k].wait_recv()
        c_of[k] = remote(
            gat.at[unit(k), pl.ds(c * 2, 2)], gat.at[unit(k), pl.ds(c * 2, 2)], cs.at[k], cr.at[k], core_peer
        )
        sent.append(c_of[k])

    def gathered(k):
        if k in c_of:
            c_of[k].wait_recv()
        for gi in range(groups):
            block = gat[k, :, pl.ds(gi * 4, 4)].reshape(256, q_width)
            moved = jnp.dot(perm[...], block, preferred_element_type=F32).astype(BF16)
            for q in range(4):
                nat[k, pl.ds(gi * 64, 64), pl.ds(q * q_width, q_width)] = moved[q * 64 : (q + 1) * 64]

    order = list(reversed(range(layers)))
    for t in order:
        z_start(t)

    row = lax.broadcasted_iota(jnp.int32, (256, 256), 0)
    col = lax.broadcasted_iota(jnp.int32, (256, 256), 1)
    perm[...] = jnp.where(natural_of(row) == col, 1.0, 0.0).astype(BF16)
    perm_t[...] = jnp.where(natural_of(col) == row, 1.0, 0.0).astype(BF16)
    act_copy.wait()

    def source_grad(s):
        pairs = [pair_index(s, t, layers) for t in range(s, layers)]
        for p in pairs:
            weight["dec", p].wait()

        def body(i, carry):
            cols = pl.ds(pl.multiple_of(i * tile, tile), tile)
            total = jnp.zeros((tokens, tile), F32)
            for t, p in zip(range(s, layers), pairs):
                total = total + lax.dot_general(nat[t], dec_v[p, cols, :], NT, preferred_element_type=F32)
            pre_v[s, :, cols] = (total * act_v[s, :, cols].astype(F32)).astype(BF16)
            return carry

        lax.fori_loop(0, local // tile, body, 0)

    out_copies = []

    def save(src, dst):
        copy = pltpu.make_async_copy(src, dst, o_sem.at[len(out_copies)])
        copy.start()
        out_copies.append(copy)

    first, second = {}, {}

    def input_partial(s):
        weight["enc", s].wait()

        def body(q, carry):
            deep = pl.ds(pl.multiple_of(q * q_width, q_width), q_width)
            part = lax.dot_general(pre_v[s], enc_v[s, deep, :], NT, preferred_element_type=F32).astype(BF16)
            for gi in range(groups):
                stage[s, gi, q] = part[gi * 64 : (gi + 1) * 64]
            return carry

        lax.fori_loop(0, 4, body, 0)
        for gi in range(groups):
            block = stage[s, gi].reshape(256, q_width)
            moved = jnp.dot(perm_t[...], block, preferred_element_type=F32).astype(BF16)
            s1[s, :, pl.ds(gi * 4, 4)] = moved.reshape(4, 4, 16, q_width)
        first[s] = remote(s1.at[s, pl.ds(2 - c * 2, 2)], r1.at[s], s1s.at[s], s1r.at[s], core_peer)
        sent.append(first[s])

    def reduce_chip(s):
        first[s].wait_recv()
        s2[s] = (s1[s, pl.ds(c * 2, 2)].astype(F32) + r1[s].astype(F32)).astype(BF16)
        second[s] = [
            remote(s2.at[s, w % 2, w // 2], r2.at[s, m], s2s.at[s, m], s2r.at[s, m], w * 2 + c)
            for m, w in enumerate(chips)
        ]
        sent.extend(second[s])
        keep[s] = s1[s, l_mine, h].astype(F32) + r1[s, y, h].astype(F32)

    def finish(s):
        total = keep[s]
        for m, copy in enumerate(second[s]):
            copy.wait_recv()
            total = total + r2[s, m].astype(F32)
        for q in range(4):
            ig_ref[s, :, pl.ds(q * q_width, q_width)] = total[q * rows : (q + 1) * rows].astype(BF16)

    def x_ready(k):
        gathered(k)
        save(nat.at[k], xg_hbm.at[k - layers])

    for t in order:
        y_start(t)
    z_start(second_unit)
    for t in order:
        c_start(t)
    for i, s in enumerate(order):
        last = i == layers - 1
        gathered(s)
        if last:
            y_start(second_unit)
        source_grad(s)
        save(pre_v.at[s], pre_hbm.at[s])
        if i >= 1:
            reduce_chip(order[i - 1])
        input_partial(s)
    s = order[-1]
    reduce_chip(s)
    c_start(second_unit)
    for t in range(layers):
        x_ready(layers + t)
    early = [copy for copy in sent if all(copy is not other for other in second[s])]
    for copy in early:
        copy.wait_send()
    for t in order:
        finish(t)
    for copy in out_copies:
        copy.wait()
    for copy in second[s]:
        copy.wait_send()


def outer_kernel(scale, x_ref, pre_ref, out_hbm, out_v, sem):
    layers, width = out_v.shape[:2]
    deep = width // 2
    copies = []
    for l in range(layers):
        for d in range(0, width, deep):
            rows = pl.ds(d, deep)
            total = lax.dot_general(x_ref[l, :, rows], pre_ref[l], TN, preferred_element_type=F32)
            out_v[l, rows, :] = (total * scale).astype(BF16)
            copy = pltpu.make_async_copy(out_v.at[l, rows], out_hbm.at[l, rows], sem.at[len(copies)])
            copy.start()
            copies.append(copy)
    for copy in copies:
        copy.wait()


def per_device(n, grad_out, layer_inputs, active, enc_weight, dec_weight):
    rows, layers, width = grad_out.shape
    local = enc_weight.shape[2]
    tokens = rows * n
    high = n // 4
    q_width = width // 4
    dma = pltpu.SemaphoreType.DMA
    pairs = dec_weight.shape[0]
    any_space = pl.BlockSpec(memory_space=pl.ANY)
    vmem = pl.BlockSpec(memory_space=pltpu.VMEM)
    macs = tokens * local * width * (pairs + layers)
    pre, xg, input_grad = pl.pallas_call(
        functools.partial(exchange_kernel, n, layers, rows, width),
        out_shape=(
            jax.ShapeDtypeStruct((layers, tokens, local), BF16),
            jax.ShapeDtypeStruct((layers, tokens, width), BF16),
            jax.ShapeDtypeStruct((layers, rows, width), BF16),
        ),
        in_specs=[vmem, vmem, any_space, any_space, any_space],
        out_specs=(any_space, any_space, vmem),
        scratch_shapes=[
            pltpu.VMEM((layers, tokens, local), jnp.int32),
            pltpu.VMEM((layers, width, local), BF16),
            pltpu.VMEM((pairs, local, width), BF16),
            pltpu.VMEM((2 * layers, 16, q_width), F32),
            pltpu.VMEM((2 * layers, 4, high, 16, q_width), BF16),
            pltpu.VMEM((2 * layers, tokens, width), BF16),
            pltpu.VMEM((layers, tokens, local), BF16),
            pltpu.VMEM((layers, n // 16, 4, 64, q_width), BF16),
            pltpu.VMEM((layers, 4, high, 16, q_width), BF16),
            pltpu.VMEM((layers, 2, high, 16, q_width), BF16),
            pltpu.VMEM((layers, 16, q_width), F32),
            pltpu.VMEM((layers, 2, high, 16, q_width), BF16),
            pltpu.VMEM((layers, 2 * high - 1, 16, q_width), BF16),
            pltpu.VMEM((256, 256), BF16),
            pltpu.VMEM((256, 256), BF16),
            dma((1 + pairs + layers,)),
            dma((2 * layers,)),
            dma((2 * layers, high - 1)),
            dma((2 * layers, high - 1)),
            dma((2 * layers,)),
            dma((2 * layers,)),
            dma((2 * layers,)),
            dma((2 * layers,)),
            dma((layers,)),
            dma((layers,)),
            dma((layers, 2 * high - 1)),
            dma((layers, 2 * high - 1)),
        ],
        compiler_params=pltpu.CompilerParams(
            collective_id=0, has_side_effects=True, vmem_limit_bytes=60 * 1024 * 1024
        ),
        cost_estimate=pl.CostEstimate(
            flops=2 * macs,
            bytes_accessed=2 * local * width * (pairs + layers),
            transcendentals=0,
        ),
    )(
        grad_out.transpose(1, 0, 2),
        layer_inputs.transpose(1, 0, 2),
        active.transpose(1, 0, 2),
        enc_weight,
        dec_weight,
    )

    enc_grad = pl.pallas_call(
        functools.partial(outer_kernel, tokens ** (-0.5)),
        in_specs=[vmem, vmem],
        out_specs=any_space,
        scratch_shapes=[pltpu.VMEM((layers, width, local), BF16), dma((2 * layers,))],
        out_shape=jax.ShapeDtypeStruct((layers, width, local), BF16),
        compiler_params=pltpu.CompilerParams(vmem_limit_bytes=60 * 1024 * 1024),
        cost_estimate=pl.CostEstimate(
            flops=2 * tokens * local * width * layers,
            bytes_accessed=2 * local * width * layers,
            transcendentals=0,
        ),
    )(xg, pre)
    return enc_grad, input_grad.transpose(1, 0, 2)


def solution(mesh):
    return jax.shard_map(
        functools.partial(per_device, mesh.shape["lat"]),
        mesh=mesh,
        in_specs=(
            P(("group", "lat"), None, None),
            P(("group", "lat"), None, None),
            P("group", None, "lat"),
            P(None, None, "lat"),
            P(None, "lat", None),
        ),
        out_specs=(P("group", None, "lat"), P(("group", "lat"), None, None)),
        check_vma=False,
    )
```

```python
import functools

import jax
import jax.numpy as jnp
from jax import lax
from jax.experimental import pallas as pl
from jax.experimental.pallas import tpu as pltpu
from jax.sharding import PartitionSpec as P

MESH = pl.DeviceIdType.MESH
F32 = jnp.float32
BF16 = jnp.bfloat16
NT = (((1,), (1,)), ((), ()))
TN = (((0,), (0,)), ((), ()))


def pair_index(source, target, layers):
    return source * layers - source * (source - 1) // 2 + target - source


def natural_of(index):
    q = index >> 6
    hh = (index >> 4) & 3
    y = (index >> 3) & 1
    c = (index >> 2) & 1
    r = index & 3
    return (c * 2 + y) * 64 + hh * 16 + q * 4 + r


def exchange_kernel(
    n, layers, rows, width,
    g_ref, x_ref, act_hbm, enc_hbm, dec_hbm,
    pre_hbm, xg_hbm, ig_ref,
    act_v, enc_v, dec_v, own32, gat, nat, pre_v, stage,
    s1, r1, keep, s2, r2, perm, perm_t,
    w_sem, o_sem, zs, zr, ys, yr, cs, cr, s1s, s1r, s2s, s2r,
):
    high = n // 4
    groups = n // 16
    tokens = rows * n
    q_width = width // 4
    local = enc_v.shape[2]
    tile = min(512, local)
    me = lax.axis_index("lat")
    group = lax.axis_index("group")
    c = me % 2
    y = (me // 2) % 2
    h = me // 4
    l_mine = c * 2 + y
    core_peer = me + 1 - 2 * c
    y_peer = me + 2 - 4 * y
    chip = me // 2
    chips = [(chip + m) % (2 * high) for m in range(1, 2 * high)]
    z_peers = [((h + j) % high) * 4 + me % 4 for j in range(1, high)]

    weight = {}
    count = 0

    def load(src, dst):
        nonlocal count
        copy = pltpu.make_async_copy(src, dst, w_sem.at[count])
        copy.start()
        count += 1
        return copy

    barrier = pltpu.get_barrier_semaphore()
    for peer in [w * 2 + c for w in chips] + [core_peer]:
        pl.semaphore_signal(barrier, inc=1, device_id=(group, peer), device_id_type=MESH)

    act_copy = load(act_hbm, act_v)
    for source in reversed(range(layers)):
        for target in range(source, layers):
            p = pair_index(source, target, layers)
            weight["dec", p] = load(dec_hbm.at[p], dec_v.at[p])
        weight["enc", source] = load(enc_hbm.at[source], enc_v.at[source])

    for a, ref in enumerate((g_ref, x_ref)):
        for t in range(layers):
            value = ref[t].astype(F32)
            for q in range(4):
                own32[a * layers + t, pl.ds(q * rows, rows), :] = value[:, q * q_width : (q + 1) * q_width]
    for k in range(2 * layers):
        gat.at[k, l_mine, h][...] = own32[k].astype(BF16)

    pl.semaphore_wait(barrier, len(chips) + 1)

    def remote(src, dst, send, recv, peer):
        copy = pltpu.make_async_remote_copy(
            src_ref=src, dst_ref=dst, send_sem=send, recv_sem=recv,
            device_id=(group, peer), device_id_type=MESH,
        )
        copy.start()
        return copy

    sent = []
    second_unit = layers

    def unit(k):
        return pl.ds(k, layers if k == second_unit else 1)

    z_of, y_of, c_of = {}, {}, {}

    def z_start(k):
        z_of[k] = [
            remote(gat.at[unit(k), l_mine, h], gat.at[unit(k), l_mine, h], zs.at[k, j], zr.at[k, j], peer)
            for j, peer in enumerate(z_peers)
        ]
        sent.extend(z_of[k])

    def y_start(k):
        for copy in z_of[k]:
            copy.wait_recv()
        y_of[k] = remote(gat.at[unit(k), l_mine], gat.at[unit(k), l_mine], ys.at[k], yr.at[k], y_peer)
        sent.append(y_of[k])

    def c_start(k):
        y_of[k].wait_recv()
        c_of[k] = remote(
            gat.at[unit(k), pl.ds(c * 2, 2)], gat.at[unit(k), pl.ds(c * 2, 2)], cs.at[k], cr.at[k], core_peer
        )
        sent.append(c_of[k])

    def gathered(k):
        if k in c_of:
            c_of[k].wait_recv()
        for gi in range(groups):
            block = gat[k, :, pl.ds(gi * 4, 4)].reshape(256, q_width)
            moved = jnp.dot(perm[...], block, preferred_element_type=F32).astype(BF16)
            for q in range(4):
                nat[k, pl.ds(gi * 64, 64), pl.ds(q * q_width, q_width)] = moved[q * 64 : (q + 1) * 64]

    order = list(reversed(range(layers)))
    for t in order:
        z_start(t)

    row = lax.broadcasted_iota(jnp.int32, (256, 256), 0)
    col = lax.broadcasted_iota(jnp.int32, (256, 256), 1)
    perm[...] = jnp.where(natural_of(row) == col, 1.0, 0.0).astype(BF16)
    perm_t[...] = jnp.where(natural_of(col) == row, 1.0, 0.0).astype(BF16)
    act_copy.wait()

    def source_grad(s):
        pairs = [pair_index(s, t, layers) for t in range(s, layers)]
        for p in pairs:
            weight["dec", p].wait()

        def body(i, carry):
            cols = pl.ds(pl.multiple_of(i * tile, tile), tile)
            total = jnp.zeros((tokens, tile), F32)
            for t, p in zip(range(s, layers), pairs):
                total = total + lax.dot_general(nat[t], dec_v[p, cols, :], NT, preferred_element_type=F32)
            pre_v[s, :, cols] = (total * act_v[s, :, cols].astype(F32)).astype(BF16)
            return carry

        lax.fori_loop(0, local // tile, body, 0, unroll=True)

    out_copies = []

    def save(src, dst):
        copy = pltpu.make_async_copy(src, dst, o_sem.at[len(out_copies)])
        copy.start()
        out_copies.append(copy)

    first, second = {}, {}

    def input_partial(s):
        weight["enc", s].wait()

        def body(q, carry):
            deep = pl.ds(pl.multiple_of(q * q_width, q_width), q_width)
            part = lax.dot_general(pre_v[s], enc_v[s, deep, :], NT, preferred_element_type=F32).astype(BF16)
            for gi in range(groups):
                stage[s, gi, q] = part[gi * 64 : (gi + 1) * 64]
            return carry

        lax.fori_loop(0, 4, body, 0, unroll=True)
        for gi in range(groups):
            block = stage[s, gi].reshape(256, q_width)
            moved = jnp.dot(perm_t[...], block, preferred_element_type=F32).astype(BF16)
            s1[s, :, pl.ds(gi * 4, 4)] = moved.reshape(4, 4, 16, q_width)
        first[s] = remote(s1.at[s, pl.ds(2 - c * 2, 2)], r1.at[s], s1s.at[s], s1r.at[s], core_peer)
        sent.append(first[s])

    def reduce_chip(s):
        first[s].wait_recv()
        s2[s] = (s1[s, pl.ds(c * 2, 2)].astype(F32) + r1[s].astype(F32)).astype(BF16)
        second[s] = [
            remote(s2.at[s, w % 2, w // 2], r2.at[s, m], s2s.at[s, m], s2r.at[s, m], w * 2 + c)
            for m, w in enumerate(chips)
        ]
        sent.extend(second[s])
        keep[s] = s1[s, l_mine, h].astype(F32) + r1[s, y, h].astype(F32)

    def finish(s):
        total = keep[s]
        for m, copy in enumerate(second[s]):
            copy.wait_recv()
            total = total + r2[s, m].astype(F32)
        for q in range(4):
            ig_ref[s, :, pl.ds(q * q_width, q_width)] = total[q * rows : (q + 1) * rows].astype(BF16)

    def x_ready(k):
        gathered(k)
        save(nat.at[k], xg_hbm.at[k - layers])

    for t in order:
        y_start(t)
    z_start(second_unit)
    for t in order:
        c_start(t)
    for i, s in enumerate(order):
        last = i == layers - 1
        gathered(s)
        if last:
            y_start(second_unit)
        source_grad(s)
        save(pre_v.at[s], pre_hbm.at[s])
        if i >= 1:
            reduce_chip(order[i - 1])
        input_partial(s)
    s = order[-1]
    reduce_chip(s)
    c_start(second_unit)
    for t in range(layers):
        x_ready(layers + t)
    early = [copy for copy in sent if all(copy is not other for other in second[s])]
    for copy in early:
        copy.wait_send()
    for t in order:
        finish(t)
    for copy in out_copies:
        copy.wait()
    for copy in second[s]:
        copy.wait_send()


def outer_kernel(scale, x_ref, pre_ref, out_hbm, out_v, sem):
    layers, width = out_v.shape[:2]
    deep = width // 2
    copies = []
    for l in range(layers):
        for d in range(0, width, deep):
            rows = pl.ds(d, deep)
            total = lax.dot_general(x_ref[l, :, rows], pre_ref[l], TN, preferred_element_type=F32)
            out_v[l, rows, :] = (total * scale).astype(BF16)
            copy = pltpu.make_async_copy(out_v.at[l, rows], out_hbm.at[l, rows], sem.at[len(copies)])
            copy.start()
            copies.append(copy)
    for copy in copies:
        copy.wait()


def per_device(n, grad_out, layer_inputs, active, enc_weight, dec_weight):
    rows, layers, width = grad_out.shape
    local = enc_weight.shape[2]
    tokens = rows * n
    high = n // 4
    q_width = width // 4
    dma = pltpu.SemaphoreType.DMA
    pairs = dec_weight.shape[0]
    any_space = pl.BlockSpec(memory_space=pl.ANY)
    vmem = pl.BlockSpec(memory_space=pltpu.VMEM)
    macs = tokens * local * width * (pairs + layers)
    pre, xg, input_grad = pl.pallas_call(
        functools.partial(exchange_kernel, n, layers, rows, width),
        out_shape=(
            jax.ShapeDtypeStruct((layers, tokens, local), BF16),
            jax.ShapeDtypeStruct((layers, tokens, width), BF16),
            jax.ShapeDtypeStruct((layers, rows, width), BF16),
        ),
        in_specs=[vmem, vmem, any_space, any_space, any_space],
        out_specs=(any_space, any_space, vmem),
        scratch_shapes=[
            pltpu.VMEM((layers, tokens, local), jnp.int32),
            pltpu.VMEM((layers, width, local), BF16),
            pltpu.VMEM((pairs, local, width), BF16),
            pltpu.VMEM((2 * layers, 16, q_width), F32),
            pltpu.VMEM((2 * layers, 4, high, 16, q_width), BF16),
            pltpu.VMEM((2 * layers, tokens, width), BF16),
            pltpu.VMEM((layers, tokens, local), BF16),
            pltpu.VMEM((layers, n // 16, 4, 64, q_width), BF16),
            pltpu.VMEM((layers, 4, high, 16, q_width), BF16),
            pltpu.VMEM((layers, 2, high, 16, q_width), BF16),
            pltpu.VMEM((layers, 16, q_width), F32),
            pltpu.VMEM((layers, 2, high, 16, q_width), BF16),
            pltpu.VMEM((layers, 2 * high - 1, 16, q_width), BF16),
            pltpu.VMEM((256, 256), BF16),
            pltpu.VMEM((256, 256), BF16),
            dma((1 + pairs + layers,)),
            dma((2 * layers,)),
            dma((2 * layers, high - 1)),
            dma((2 * layers, high - 1)),
            dma((2 * layers,)),
            dma((2 * layers,)),
            dma((2 * layers,)),
            dma((2 * layers,)),
            dma((layers,)),
            dma((layers,)),
            dma((layers, 2 * high - 1)),
            dma((layers, 2 * high - 1)),
        ],
        compiler_params=pltpu.CompilerParams(
            collective_id=0, has_side_effects=True, vmem_limit_bytes=60 * 1024 * 1024
        ),
        cost_estimate=pl.CostEstimate(
            flops=2 * macs,
            bytes_accessed=2 * local * width * (pairs + layers),
            transcendentals=0,
        ),
    )(
        grad_out.transpose(1, 0, 2),
        layer_inputs.transpose(1, 0, 2),
        active.transpose(1, 0, 2),
        enc_weight,
        dec_weight,
    )

    enc_grad = pl.pallas_call(
        functools.partial(outer_kernel, tokens ** (-0.5)),
        in_specs=[vmem, vmem],
        out_specs=any_space,
        scratch_shapes=[pltpu.VMEM((layers, width, local), BF16), dma((2 * layers,))],
        out_shape=jax.ShapeDtypeStruct((layers, width, local), BF16),
        compiler_params=pltpu.CompilerParams(vmem_limit_bytes=60 * 1024 * 1024),
        cost_estimate=pl.CostEstimate(
            flops=2 * tokens * local * width * layers,
            bytes_accessed=2 * local * width * layers,
            transcendentals=0,
        ),
    )(xg, pre)
    return enc_grad, input_grad.transpose(1, 0, 2)


def solution(mesh):
    return jax.shard_map(
        functools.partial(per_device, mesh.shape["lat"]),
        mesh=mesh,
        in_specs=(
            P(("group", "lat"), None, None),
            P(("group", "lat"), None, None),
            P("group", None, "lat"),
            P(None, None, "lat"),
            P(None, "lat", None),
        ),
        out_specs=(P("group", None, "lat"), P(("group", "lat"), None, None)),
        check_vma=False,
    )
```
